32 devices in a mesh: blk: 8 (over y, x, core), wide: 4 (over z).
Axes of the slice: x: 2, y: 2, z: 4, core: 2. Of those that a mesh axis runs over, the one named last changes fastest.
Arguments:
- vectors: bfloat16 [16, 4096], P(None, ('blk', 'wide')), may hold values from -6 to 6
- blocks: bfloat16 [32, 4, 16, 128, 128], P(('blk', 'wide')), may hold values from -0.046875 to 0.046875
- columns: int32 [32, 4, 16], P(('blk', 'wide')), may hold values from 0 to 3
- counts: int32 [32, 4], P(('blk', 'wide')), may hold values from 1 to 16, as said below
Outputs:
- product: float32 [16, 4096], P(None, ('blk', 'wide'))
The draws below stay inside these ranges and needn't reach their ends.
Inputs may be any that keep to these rules, and one draw needn't show every extreme that they name: `counts`: every block row has at least one live slot in every step; some block row fills all 16 slots of some step.
All inputs are finite; a program needn't handle non-finite values.
Results may differ from the reference program's by a relative error of at most 0.0003.
Values may be sent and summed in bfloat16 or wider, within the bound.
A program may use at most 64 MiB of HBM per device.

```python
import jax
import jax.numpy as jnp
from jax import lax

STATES_PER_BLOCK = 128
K = 16
ROW_BLOCKS_LOCAL = 1
STORED_SLOTS = 16
HALF_GROUPS = 4
GROUP_BLOCKS = 4
TOTAL_BLOCKS = 32
N = 4096
N_BLK = 8
N_WIDE = 4


def draw_counts(key, part):
    height_key, discard_key, key_fill = jax.random.split(key, 3)
    device_total = TOTAL_BLOCKS // ROW_BLOCKS_LOCAL
    height_value = jax.random.randint(height_key, (device_total, 1, 1), 1, STORED_SLOTS + 1)
    discard_flag = jax.random.randint(discard_key, (device_total, ROW_BLOCKS_LOCAL, HALF_GROUPS), 0, STORED_SLOTS)
    entry_values = height_value - discard_flag % (height_value // 2 + 1)
    entry_values = entry_values.reshape(TOTAL_BLOCKS * HALF_GROUPS)
    full_selector = jax.random.randint(key_fill, (), 0, TOTAL_BLOCKS * HALF_GROUPS)
    entry_values = entry_values.at[full_selector].set(STORED_SLOTS)
    return entry_values.reshape(TOTAL_BLOCKS, HALF_GROUPS).astype(jnp.int32)


def place_ends(array, rng, least, high):
    index_at = [jax.random.randint(jax.random.fold_in(rng, axis), (), 0, length) for axis, length in enumerate(array.shape)]
    longest = array.shape.index(max(array.shape))
    next_to = index_at[:longest] + [(index_at[longest] + 1) % array.shape[longest]] + index_at[longest + 1:]
    return array.at[tuple(index_at)].set(least).at[tuple(next_to)].set(high)


def shard_levels(key, extent, pieces, least, top_value):
    def one(dim, shards_of):
        steps = jax.random.uniform(jax.random.fold_in(jax.random.fold_in(key, 6), dim), (shards_of,), jnp.float32, least / len(pieces), top_value / len(pieces))
        return jnp.repeat(jnp.exp(steps), extent[dim] // shards_of).reshape((-1,) + (1,) * (len(extent) - dim - 1))

    level = one(*pieces[0])
    for cut in pieces[1:]:
        level = level * one(*cut)
    return level


def centred(key, shape, spread, most, pieces=(), kind=jnp.bfloat16):
    loudness = shard_levels(key, shape, pieces, -0.22, 0.18) if pieces else 1.0
    entries = jax.random.normal(key, shape, jnp.float32) * spread * loudness
    return jnp.minimum(jnp.maximum(entries, -most), most).astype(kind)


def setup_inputs(seed: int = 0) -> dict:
    key_list = jax.random.split(jax.random.key(seed), 5)
    vectors = centred(key_list[0], (K, N), 1.0, 6.0, ((1, 32),))
    blocks = centred(key_list[1], (TOTAL_BLOCKS, HALF_GROUPS, STORED_SLOTS, STATES_PER_BLOCK, STATES_PER_BLOCK), (2 * HALF_GROUPS * STORED_SLOTS * STATES_PER_BLOCK) ** -0.5, 0.046875, ((0, 32),))
    columns = place_ends(jax.random.randint(key_list[2], (TOTAL_BLOCKS, HALF_GROUPS, STORED_SLOTS), 0, GROUP_BLOCKS), jax.random.fold_in(key_list[2], 1), 0, GROUP_BLOCKS - 1).astype(jnp.int32)
    counts = draw_counts(jax.random.fold_in(key_list[4], 71), 0)
    return {"vectors": vectors, "blocks": blocks, "columns": columns, "counts": counts}


def reference(vectors, blocks, columns, counts):
    vec_count = vectors.shape[0]
    block_rows = blocks.shape[0]
    grid = vectors.astype(jnp.float32).reshape(vec_count, block_rows, STATES_PER_BLOCK)
    slot_sequence = jnp.arange(STORED_SLOTS, dtype=jnp.int32)
    step_iota = jnp.arange(HALF_GROUPS, dtype=jnp.int32)

    def one_row(accum, row_index):
        group = (row_index // ROW_BLOCKS_LOCAL) // N_WIDE
        base = ((group + step_iota) % N_BLK) * GROUP_BLOCKS
        global_cols = (base[:, None] + columns[row_index]).astype(jnp.int32)
        live = (slot_sequence[None, :] < counts[row_index][:, None]).astype(jnp.float32)
        tiles = blocks[row_index].astype(jnp.float32) * live[:, :, None, None]
        picked = grid[:, global_cols, :]
        direct = jnp.einsum("sjic,ksjc->ki", tiles, picked, precision=lax.Precision.HIGHEST)
        own_rows = grid[:, row_index, :]
        transposed = jnp.einsum("sjic,ki->ksjc", tiles, own_rows, precision=lax.Precision.HIGHEST)
        accum = accum.at[:, global_cols, :].add(transposed)
        return accum, direct

    start = jnp.zeros((vec_count, block_rows, STATES_PER_BLOCK), jnp.float32)
    accum, directs = lax.scan(one_row, start, jnp.arange(block_rows, dtype=jnp.int32))
    result = jnp.transpose(directs, (1, 0, 2)) + accum
    return result.reshape(vec_count, block_rows * STATES_PER_BLOCK)
```

```python
import functools

import jax
import jax.numpy as jnp
from jax import lax
from jax.experimental import pallas as pl
from jax.experimental.pallas import tpu as pltpu
from jax.sharding import PartitionSpec as P

MESH = pl.DeviceIdType.MESH


def kernel(groups, wide, steps, cols, counts, vec, blocks, out, *scratch):
    panels = scratch[:steps]
    tiles = scratch[steps : 2 * steps]
    (parts, landed, total, shares, load_sem, a_send, a_recv, b_send, b_recv,
     p_send, p_recv, z_send, z_recv) = scratch[2 * steps :]
    slots = blocks.shape[2]
    size = blocks.shape[3]
    vecs = vec.shape[0]
    g = lax.axis_index("blk")
    w = lax.axis_index("wide")

    def group(offset):
        return (lax.rem(g + (offset + groups), groups), w)

    def owner(offset):
        return (g, lax.rem(w + offset, wide))

    order = [*range(1, steps), 0]
    loads = {}
    for s in order:
        loads[s] = pltpu.make_async_copy(blocks.at[0, s], tiles[s], load_sem.at[s])
        loads[s].start()

    barrier = pltpu.get_barrier_semaphore()
    peers = [owner(d) for d in range(1, wide)]
    for d in range(1, steps):
        peers += [group(d), group(-d)]
    for peer in peers:
        pl.semaphore_signal(barrier, inc=1, device_id=peer, device_id_type=MESH)
    panels[0][w] = vec[...]
    pl.semaphore_wait(barrier, len(peers))

    def remote(src, dst, send, recv, to):
        return pltpu.make_async_remote_copy(
            src_ref=src, dst_ref=dst, send_sem=send, recv_sem=recv, device_id=to, device_id_type=MESH
        )

    spread = [
        remote(vec, panels[0].at[w], a_send.at[d - 1], a_recv.at[d - 1], owner(d))
        for d in range(1, wide)
    ]
    for c in spread:
        c.start()

    own = vec[...]
    none = jnp.zeros_like(own)

    def live(s, j):
        return j < counts[0, s]

    def transposed(s):
        loads[s].wait()
        left = []
        for j in range(slots):
            code = jnp.where(live(s, j), cols[0, s, j], -1)
            left.append(
                jnp.concatenate([jnp.where(code == n, own, none) for n in range(wide)], axis=0)
            )
        left = jnp.concatenate(left, axis=1)
        part = jnp.dot(
            left, tiles[s][...].reshape(slots * size, size), preferred_element_type=jnp.float32
        )
        parts[s] = part.reshape(wide, vecs, size)

    def direct(s):
        left = [jnp.where(live(s, j), panels[s][cols[0, s, j]], none) for j in range(slots)]
        left = jnp.concatenate(left, axis=1)
        right = jnp.concatenate([tiles[s][j] for j in range(slots)], axis=1)
        return lax.dot_general(
            left, right, (((1,), (1,)), ((), ())), preferred_element_type=jnp.float32
        )

    passed, handed = [], []
    for s in order:
        transposed(s)
        if s:
            c = remote(parts.at[s], landed.at[s - 1], p_send.at[s - 1], p_recv.at[s - 1], group(s))
            c.start()
            handed.append(c)
        if s == 1:
            for c in spread:
                c.wait_recv()
            for d in range(1, steps):
                c = remote(panels[0], panels[d], b_send.at[d - 1], b_recv.at[d - 1], group(-d))
                c.start()
                passed.append(c)

    answer = direct(0)
    for s in range(1, steps):
        passed[s - 1].wait_recv()
        answer += direct(s)

    summed = parts[0]
    for s in range(1, steps):
        handed[s - 1].wait_recv()
        summed += landed[s - 1]
    total[...] = summed
    returned = []
    for d in range(1, wide):
        to = owner(d)
        c = remote(total.at[to[1]], shares.at[d - 1], z_send.at[d - 1], z_recv.at[d - 1], to)
        c.start()
        returned.append(c)
    answer += total[w]
    for d in range(1, wide):
        returned[d - 1].wait_recv()
        answer += shares[d - 1]
    out[...] = answer
    for c in (*spread, *passed, *handed, *returned):
        c.wait_send()


def shards(mesh, vectors, blocks, columns, counts):
    groups, wide = mesh.shape["blk"], mesh.shape["wide"]
    vecs, size = vectors.shape
    _, steps, slots = blocks.shape[:3]
    sems = pltpu.SemaphoreType.DMA
    return pl.pallas_call(
        functools.partial(kernel, groups, wide, steps),
        out_shape=jax.ShapeDtypeStruct((vecs, size), jnp.float32),
        in_specs=[
            pl.BlockSpec(memory_space=pltpu.SMEM),
            pl.BlockSpec(memory_space=pltpu.SMEM),
            pl.BlockSpec(memory_space=pltpu.VMEM),
            pl.BlockSpec(memory_space=pl.ANY),
        ],
        out_specs=pl.BlockSpec(memory_space=pltpu.VMEM),
        scratch_shapes=[
            *[pltpu.VMEM((wide, vecs, size), jnp.bfloat16)] * steps,
            *[pltpu.VMEM((slots, size, size), jnp.bfloat16)] * steps,
            pltpu.VMEM((steps, wide, vecs, size), jnp.float32),
            pltpu.VMEM((steps - 1, wide, vecs, size), jnp.float32),
            pltpu.VMEM((wide, vecs, size), jnp.float32),
            pltpu.VMEM((wide - 1, vecs, size), jnp.float32),
            sems((steps,)),
            sems((wide - 1,)),
            sems((wide - 1,)),
            sems((steps - 1,)),
            sems((steps - 1,)),
            sems((steps - 1,)),
            sems((steps - 1,)),
            sems((wide - 1,)),
            sems((wide - 1,)),
        ],
        compiler_params=pltpu.CompilerParams(
            collective_id=0, has_side_effects=True, vmem_limit_bytes=14 << 20
        ),
    )(columns, counts, vectors, blocks)


def solution(mesh):
    return jax.shard_map(
        functools.partial(shards, mesh),
        mesh=mesh,
        in_specs=(
            P(None, ("blk", "wide")),
            P(("blk", "wide"), None, None, None, None),
            P(("blk", "wide"), None, None),
            P(("blk", "wide"), None),
        ),
        out_specs=P(None, ("blk", "wide")),
        check_vma=False,
    )
```

```python
import functools

import jax
import jax.numpy as jnp
from jax import lax
from jax.experimental import pallas as pl
from jax.experimental.pallas import tpu as pltpu
from jax.sharding import PartitionSpec as P

MESH = pl.DeviceIdType.MESH


def kernel(groups, wide, steps, cols_in, counts_in, vec_in, blocks, out, *scratch):
    panels = scratch[:steps]
    tiles = scratch[steps : 2 * steps]
    (cols, counts, vec, parts, landed, total, shares, in_sem, load_sem, a_send, a_recv, b_send, b_recv,
     p_send, p_recv, z_send, z_recv) = scratch[2 * steps :]
    slots = blocks.shape[2]
    size = blocks.shape[3]
    vecs = vec_in.shape[0]
    g = lax.axis_index("blk")
    w = lax.axis_index("wide")

    def group(offset):
        return (lax.rem(g + (offset + groups), groups), w)

    def owner(offset):
        return (g, lax.rem(w + offset, wide))

    small = [
        pltpu.make_async_copy(src, dst, in_sem.at[i])
        for i, (src, dst) in enumerate(((vec_in, vec), (cols_in, cols), (counts_in, counts)))
    ]
    for c in small:
        c.start()
    order = [*range(1, steps), 0]
    loads = {}
    for s in order:
        loads[s] = pltpu.make_async_copy(blocks.at[0, s], tiles[s], load_sem.at[s])
        loads[s].start()

    barrier = pltpu.get_barrier_semaphore()
    peers = [owner(d) for d in range(1, wide)]
    for d in range(1, steps):
        peers += [group(d), group(-d)]
    for peer in peers:
        pl.semaphore_signal(barrier, inc=1, device_id=peer, device_id_type=MESH)
    small[0].wait()
    panels[0][w] = vec[...]
    pl.semaphore_wait(barrier, len(peers))

    def remote(src, dst, send, recv, to):
        return pltpu.make_async_remote_copy(
            src_ref=src, dst_ref=dst, send_sem=send, recv_sem=recv, device_id=to, device_id_type=MESH
        )

    spread = [
        remote(vec, panels[0].at[w], a_send.at[d - 1], a_recv.at[d - 1], owner(d))
        for d in range(1, wide)
    ]
    for c in spread:
        c.start()

    for c in small[1:]:
        c.wait()
    own = vec[...]
    none = jnp.zeros_like(own)

    def live(s, j):
        return j < counts[0, s]

    def transposed(s):
        loads[s].wait()
        left = []
        for j in range(slots):
            code = jnp.where(live(s, j), cols[0, s, j], -1)
            left.append(
                jnp.concatenate([jnp.where(code == n, own, none) for n in range(wide)], axis=0)
            )
        left = jnp.concatenate(left, axis=1)
        part = jnp.dot(
            left, tiles[s][...].reshape(slots * size, size), preferred_element_type=jnp.float32
        )
        parts[s] = part.reshape(wide, vecs, size)

    def direct(s):
        left = [jnp.where(live(s, j), panels[s][cols[0, s, j]], none) for j in range(slots)]
        left = jnp.concatenate(left, axis=1)
        right = jnp.concatenate([tiles[s][j] for j in range(slots)], axis=1)
        return lax.dot_general(
            left, right, (((1,), (1,)), ((), ())), preferred_element_type=jnp.float32
        )

    passed, handed = [], []
    for s in order:
        transposed(s)
        if s:
            c = remote(parts.at[s], landed.at[s - 1], p_send.at[s - 1], p_recv.at[s - 1], group(s))
            c.start()
            handed.append(c)
        if s == 1:
            for c in spread:
                c.wait_recv()
            for d in range(1, steps):
                c = remote(panels[0], panels[d], b_send.at[d - 1], b_recv.at[d - 1], group(-d))
                c.start()
                passed.append(c)

    answer = direct(0)
    for s in range(1, steps):
        passed[s - 1].wait_recv()
        answer += direct(s)

    summed = parts[0]
    for s in range(1, steps):
        handed[s - 1].wait_recv()
        summed += landed[s - 1]
    total[...] = summed
    returned = []
    for d in range(1, wide):
        to = owner(d)
        c = remote(total.at[to[1]], shares.at[d - 1], z_send.at[d - 1], z_recv.at[d - 1], to)
        c.start()
        returned.append(c)
    answer += total[w]
    for d in range(1, wide):
        returned[d - 1].wait_recv()
        answer += shares[d - 1]
    out[...] = answer
    for c in (*spread, *passed, *handed, *returned):
        c.wait_send()


def shards(mesh, vectors, blocks, columns, counts):
    groups, wide = mesh.shape["blk"], mesh.shape["wide"]
    vecs, size = vectors.shape
    _, steps, slots = blocks.shape[:3]
    sems = pltpu.SemaphoreType.DMA
    return pl.pallas_call(
        functools.partial(kernel, groups, wide, steps),
        out_shape=jax.ShapeDtypeStruct((vecs, size), jnp.float32),
        in_specs=[pl.BlockSpec(memory_space=pltpu.HBM)] * 4,
        out_specs=pl.BlockSpec(memory_space=pltpu.VMEM),
        scratch_shapes=[
            *[pltpu.VMEM((wide, vecs, size), jnp.bfloat16)] * steps,
            *[pltpu.VMEM((slots, size, size), jnp.bfloat16)] * steps,
            pltpu.SMEM(columns.shape, jnp.int32),
            pltpu.SMEM(counts.shape, jnp.int32),
            pltpu.VMEM((vecs, size), jnp.bfloat16),
            pltpu.VMEM((steps, wide, vecs, size), jnp.float32),
            pltpu.VMEM((steps - 1, wide, vecs, size), jnp.float32),
            pltpu.VMEM((wide, vecs, size), jnp.float32),
            pltpu.VMEM((wide - 1, vecs, size), jnp.float32),
            sems((3,)),
            sems((steps,)),
            sems((wide - 1,)),
            sems((wide - 1,)),
            sems((steps - 1,)),
            sems((steps - 1,)),
            sems((steps - 1,)),
            sems((steps - 1,)),
            sems((wide - 1,)),
            sems((wide - 1,)),
        ],
        compiler_params=pltpu.CompilerParams(
            collective_id=0, has_side_effects=True, vmem_limit_bytes=60 << 20
        ),
    )(columns, counts, vectors, blocks)


def solution(mesh):
    return jax.shard_map(
        functools.partial(shards, mesh),
        mesh=mesh,
        in_specs=(
            P(None, ("blk", "wide")),
            P(("blk", "wide"), None, None, None, None),
            P(("blk", "wide"), None, None),
            P(("blk", "wide"), None),
        ),
        out_specs=P(None, ("blk", "wide")),
        check_vma=False,
    )
```

```python
import functools

import jax
import jax.numpy as jnp
from jax import lax
from jax.experimental import pallas as pl
from jax.experimental.pallas import tpu as pltpu
from jax.sharding import PartitionSpec as P

MESH = pl.DeviceIdType.MESH


def kernel(groups, wide, steps, cols_in, counts_in, vec_in, blocks, out, *scratch):
    panels = scratch[:steps]
    tiles = scratch[steps : 2 * steps]
    (cols, counts, vec, parts, landed, total, shares, in_sem, load_sem, a_send, a_recv, b_send, b_recv,
     p_send, p_recv, z_send, z_recv) = scratch[2 * steps :]
    slots = blocks.shape[2]
    size = blocks.shape[3]
    vecs = vec_in.shape[0]
    g = lax.axis_index("blk")
    w = lax.axis_index("wide")

    def group(offset):
        return (lax.rem(g + (offset + groups), groups), w)

    def owner(offset):
        return (g, lax.rem(w + offset, wide))

    small = [
        pltpu.make_async_copy(src, dst, in_sem.at[i])
        for i, (src, dst) in enumerate(((vec_in, vec), (cols_in, cols), (counts_in, counts)))
    ]
    for c in small:
        c.start()
    order = [*range(1, steps), 0]
    loads = {}
    for s in order:
        loads[s] = pltpu.make_async_copy(blocks.at[0, s], tiles[s], load_sem.at[s])
        loads[s].start()

    barrier = pltpu.get_barrier_semaphore()
    peers = [owner(d) for d in range(1, wide)]
    for d in range(1, steps):
        peers += [group(d), group(-d)]
    for peer in peers:
        pl.semaphore_signal(barrier, inc=1, device_id=peer, device_id_type=MESH)
    small[0].wait()
    panels[0][w] = vec[...]
    pl.semaphore_wait(barrier, len(peers))

    def remote(src, dst, send, recv, to):
        return pltpu.make_async_remote_copy(
            src_ref=src, dst_ref=dst, send_sem=send, recv_sem=recv, device_id=to, device_id_type=MESH
        )

    spread = [
        remote(vec, panels[0].at[w], a_send.at[d - 1], a_recv.at[d - 1], owner(d))
        for d in range(1, wide)
    ]
    for c in spread:
        c.start()

    for c in small[1:]:
        c.wait()
    own = vec[...]
    none = jnp.zeros_like(own)

    def live(s, j):
        return j < counts[0, s]

    def transposed(s):
        loads[s].wait()
        left = []
        for j in range(slots):
            code = jnp.where(live(s, j), cols[0, s, j], -1)
            left.append(
                jnp.concatenate([jnp.where(code == n, own, none) for n in range(wide)], axis=0)
            )
        left = jnp.concatenate(left, axis=1)
        part = jnp.dot(
            left, tiles[s][...].reshape(slots * size, size), preferred_element_type=jnp.float32
        )
        parts[s] = part.reshape(wide, vecs, size)

    def direct(s):
        left = [jnp.where(live(s, j), panels[s][cols[0, s, j]], none) for j in range(slots)]
        left = jnp.concatenate(left, axis=1)
        right = jnp.concatenate([tiles[s][j] for j in range(slots)], axis=1)
        return lax.dot_general(
            left, right, (((1,), (1,)), ((), ())), preferred_element_type=jnp.float32
        )

    passed, handed = [], []
    for s in order:
        transposed(s)
        if s:
            c = remote(parts.at[s], landed.at[s - 1], p_send.at[s - 1], p_recv.at[s - 1], group(s))
            c.start()
            handed.append(c)

    for c in spread:
        c.wait_recv()
    for d in range(1, steps):
        c = remote(panels[0], panels[d], b_send.at[d - 1], b_recv.at[d - 1], group(-d))
        c.start()
        passed.append(c)

    answer = direct(0)
    summed = parts[0]
    for s in range(1, steps):
        handed[s - 1].wait_recv()
        summed += landed[s - 1]
    total[...] = summed
    returned = []
    for d in range(1, wide):
        to = owner(d)
        c = remote(total.at[to[1]], shares.at[d - 1], z_send.at[d - 1], z_recv.at[d - 1], to)
        c.start()
        returned.append(c)
    answer += total[w]
    for s in range(1, steps):
        passed[s - 1].wait_recv()
        answer += direct(s)
    for d in range(1, wide):
        returned[d - 1].wait_recv()
        answer += shares[d - 1]
    out[...] = answer
    for c in (*spread, *passed, *handed, *returned):
        c.wait_send()


def shards(mesh, vectors, blocks, columns, counts):
    groups, wide = mesh.shape["blk"], mesh.shape["wide"]
    vecs, size = vectors.shape
    _, steps, slots = blocks.shape[:3]
    sems = pltpu.SemaphoreType.DMA
    return pl.pallas_call(
        functools.partial(kernel, groups, wide, steps),
        out_shape=jax.ShapeDtypeStruct((vecs, size), jnp.float32),
        in_specs=[pl.BlockSpec(memory_space=pltpu.HBM)] * 4,
        out_specs=pl.BlockSpec(memory_space=pltpu.VMEM),
        scratch_shapes=[
            *[pltpu.VMEM((wide, vecs, size), jnp.bfloat16)] * steps,
            *[pltpu.VMEM((slots, size, size), jnp.bfloat16)] * steps,
            pltpu.SMEM(columns.shape, jnp.int32),
            pltpu.SMEM(counts.shape, jnp.int32),
            pltpu.VMEM((vecs, size), jnp.bfloat16),
            pltpu.VMEM((steps, wide, vecs, size), jnp.float32),
            pltpu.VMEM((steps - 1, wide, vecs, size), jnp.float32),
            pltpu.VMEM((wide, vecs, size), jnp.float32),
            pltpu.VMEM((wide - 1, vecs, size), jnp.float32),
            sems((3,)),
            sems((steps,)),
            sems((wide - 1,)),
            sems((wide - 1,)),
            sems((steps - 1,)),
            sems((steps - 1,)),
            sems((steps - 1,)),
            sems((steps - 1,)),
            sems((wide - 1,)),
            sems((wide - 1,)),
        ],
        compiler_params=pltpu.CompilerParams(
            collective_id=0, has_side_effects=True, vmem_limit_bytes=60 << 20
        ),
    )(columns, counts, vectors, blocks)


def solution(mesh):
    return jax.shard_map(
        functools.partial(shards, mesh),
        mesh=mesh,
        in_specs=(
            P(None, ("blk", "wide")),
            P(("blk", "wide"), None, None, None, None),
            P(("blk", "wide"), None, None),
            P(("blk", "wide"), None),
        ),
        out_specs=P(None, ("blk", "wide")),
        check_vma=False,
    )
```

```python
import functools

import jax
import jax.numpy as jnp
from jax import lax
from jax.experimental import pallas as pl
from jax.experimental.pallas import tpu as pltpu
from jax.sharding import PartitionSpec as P

MESH = pl.DeviceIdType.MESH


def kernel(groups, wide, steps, cols_in, counts_in, vec_in, blocks, out, *scratch):
    panels = scratch[:steps]
    tiles = scratch[steps : 2 * steps]
    (cols, counts, vec, parts, landed, total, shares, in_sem, load_sem, a_send, a_recv, b_send, b_recv,
     p_send, p_recv, z_send, z_recv) = scratch[2 * steps :]
    slots = blocks.shape[2]
    size = blocks.shape[3]
    vecs = vec_in.shape[0]
    g = lax.axis_index("blk")
    w = lax.axis_index("wide")

    def group(offset):
        return (lax.rem(g + (offset + groups), groups), w)

    def owner(offset):
        return (g, lax.rem(w + offset, wide))

    small = [
        pltpu.make_async_copy(src, dst, in_sem.at[i])
        for i, (src, dst) in enumerate(((vec_in, vec), (cols_in, cols), (counts_in, counts)))
    ]
    for c in small:
        c.start()
    order = [*range(1, steps), 0]
    loads = {}
    for s in order:
        loads[s] = pltpu.make_async_copy(blocks.at[0, s], tiles[s], load_sem.at[s])
        loads[s].start()

    barrier = pltpu.get_barrier_semaphore()
    peers = [owner(d) for d in range(1, wide)]
    for d in range(1, steps):
        peers += [group(d), group(-d)]
    for peer in peers:
        pl.semaphore_signal(barrier, inc=1, device_id=peer, device_id_type=MESH)
    small[0].wait()
    panels[0][w] = vec[...]
    pl.semaphore_wait(barrier, len(peers))

    def remote(src, dst, send, recv, to):
        return pltpu.make_async_remote_copy(
            src_ref=src, dst_ref=dst, send_sem=send, recv_sem=recv, device_id=to, device_id_type=MESH
        )

    spread = [
        remote(vec, panels[0].at[w], a_send.at[d - 1], a_recv.at[d - 1], owner(d))
        for d in range(1, wide)
    ]
    for c in spread:
        c.start()

    for c in small[1:]:
        c.wait()
    own = vec[...]
    none = jnp.zeros_like(own)

    def live(s, j):
        return j < counts[0, s]

    def transposed(s):
        loads[s].wait()
        left = []
        for j in range(slots):
            code = jnp.where(live(s, j), cols[0, s, j], -1)
            left.append(
                jnp.concatenate([jnp.where(code == n, own, none) for n in range(wide)], axis=0)
            )
        left = jnp.concatenate(left, axis=1)
        part = jnp.dot(
            left, tiles[s][...].reshape(slots * size, size), preferred_element_type=jnp.float32
        )
        parts[s] = part.reshape(wide, vecs, size)

    def direct(s):
        left = [jnp.where(live(s, j), panels[s][cols[0, s, j]], none) for j in range(slots)]
        left = jnp.concatenate(left, axis=1)
        right = jnp.concatenate([tiles[s][j] for j in range(slots)], axis=1)
        return lax.dot_general(
            left, right, (((1,), (1,)), ((), ())), preferred_element_type=jnp.float32
        )

    passed, handed = [], []
    for s in order:
        transposed(s)
        if s:
            c = remote(parts.at[s], landed.at[s - 1], p_send.at[s - 1], p_recv.at[s - 1], group(s))
            c.start()
            handed.append(c)

    for c in spread:
        c.wait_recv()
    for d in range(1, steps):
        c = remote(panels[0], panels[d], b_send.at[d - 1], b_recv.at[d - 1], group(-d))
        c.start()
        passed.append(c)

    summed = parts[0]
    for s in range(1, steps):
        handed[s - 1].wait_recv()
        summed += landed[s - 1]
    total[...] = summed
    returned = []
    for d in range(1, wide):
        to = owner(d)
        c = remote(total.at[to[1]], shares.at[d - 1], z_send.at[d - 1], z_recv.at[d - 1], to)
        c.start()
        returned.append(c)
    answer = direct(0) + total[w]
    for s in range(1, steps):
        passed[s - 1].wait_recv()
        answer += direct(s)
    for d in range(1, wide):
        returned[d - 1].wait_recv()
        answer += shares[d - 1]
    out[...] = answer
    for c in (*spread, *passed, *handed, *returned):
        c.wait_send()


def shards(mesh, vectors, blocks, columns, counts):
    groups, wide = mesh.shape["blk"], mesh.shape["wide"]
    vecs, size = vectors.shape
    _, steps, slots = blocks.shape[:3]
    sems = pltpu.SemaphoreType.DMA
    return pl.pallas_call(
        functools.partial(kernel, groups, wide, steps),
        out_shape=pltpu.VMEM((vecs, size), jnp.float32),
        in_specs=[pl.BlockSpec(memory_space=pltpu.HBM)] * 4,
        out_specs=pl.BlockSpec(memory_space=pltpu.VMEM),
        scratch_shapes=[
            *[pltpu.VMEM((wide, vecs, size), jnp.bfloat16)] * steps,
            *[pltpu.VMEM((slots, size, size), jnp.bfloat16)] * steps,
            pltpu.SMEM(columns.shape, jnp.int32),
            pltpu.SMEM(counts.shape, jnp.int32),
            pltpu.VMEM((vecs, size), jnp.bfloat16),
            pltpu.VMEM((steps, wide, vecs, size), jnp.float32),
            pltpu.VMEM((steps - 1, wide, vecs, size), jnp.float32),
            pltpu.VMEM((wide, vecs, size), jnp.float32),
            pltpu.VMEM((wide - 1, vecs, size), jnp.float32),
            sems((3,)),
            sems((steps,)),
            sems((wide - 1,)),
            sems((wide - 1,)),
            sems((steps - 1,)),
            sems((steps - 1,)),
            sems((steps - 1,)),
            sems((steps - 1,)),
            sems((wide - 1,)),
            sems((wide - 1,)),
        ],
        compiler_params=pltpu.CompilerParams(
            collective_id=0, has_side_effects=True, vmem_limit_bytes=60 << 20
        ),
    )(columns, counts, vectors, blocks)


def solution(mesh):
    return jax.shard_map(
        functools.partial(shards, mesh),
        mesh=mesh,
        in_specs=(
            P(None, ("blk", "wide")),
            P(("blk", "wide"), None, None, None, None),
            P(("blk", "wide"), None, None),
            P(("blk", "wide"), None),
        ),
        out_specs=P(None, ("blk", "wide")),
        check_vma=False,
    )
```

```python
import functools

import jax
import jax.numpy as jnp
from jax import lax
from jax.experimental import pallas as pl
from jax.experimental.pallas import tpu as pltpu
from jax.sharding import PartitionSpec as P

MESH = pl.DeviceIdType.MESH


def kernel(groups, wide, steps, cols_in, counts_in, vec_in, blocks, out, *scratch):
    panels = scratch[:steps]
    tiles = scratch[steps : 2 * steps]
    (cols, counts, vec, parts, landed, total, shares, in_sem, load_sem, a_send, a_recv, b_send, b_recv,
     p_send, p_recv, z_send, z_recv) = scratch[2 * steps :]
    slots = blocks.shape[2]
    size = blocks.shape[3]
    vecs = vec_in.shape[0]
    g = lax.axis_index("blk")
    w = lax.axis_index("wide")

    def group(offset):
        return (lax.rem(g + (offset + groups), groups), w)

    def owner(offset):
        return (g, lax.rem(w + offset, wide))

    barrier = pltpu.get_barrier_semaphore()
    peers = [owner(d) for d in range(1, wide)]
    for d in range(1, steps):
        peers += [group(d), group(-d)]
    for peer in peers:
        pl.semaphore_signal(barrier, inc=1, device_id=peer, device_id_type=MESH)

    small = [
        pltpu.make_async_copy(src, dst, in_sem.at[i])
        for i, (src, dst) in enumerate(((vec_in, vec), (cols_in, cols), (counts_in, counts)))
    ]
    for c in small:
        c.start()
    order = [*range(1, steps), 0]
    loads = {}
    for s in order:
        loads[s] = pltpu.make_async_copy(blocks.at[0, s], tiles[s], load_sem.at[s])
        loads[s].start()

    small[0].wait()
    panels[0][w] = vec[...]
    pl.semaphore_wait(barrier, len(peers))

    def remote(src, dst, send, recv, to):
        return pltpu.make_async_remote_copy(
            src_ref=src, dst_ref=dst, send_sem=send, recv_sem=recv, device_id=to, device_id_type=MESH
        )

    spread = [
        remote(vec, panels[0].at[w], a_send.at[d - 1], a_recv.at[d - 1], owner(d))
        for d in range(1, wide)
    ]
    for c in spread:
        c.start()

    for c in small[1:]:
        c.wait()
    own = vec[...]
    none = jnp.zeros_like(own)

    def live(s, j):
        return j < counts[0, s]

    def transposed(s):
        loads[s].wait()
        left = []
        for j in range(slots):
            code = jnp.where(live(s, j), cols[0, s, j], -1)
            left.append(
                jnp.concatenate([jnp.where(code == n, own, none) for n in range(wide)], axis=0)
            )
        left = jnp.concatenate(left, axis=1)
        part = jnp.dot(
            left, tiles[s][...].reshape(slots * size, size), preferred_element_type=jnp.float32
        )
        parts[s] = part.reshape(wide, vecs, size)

    def direct(s):
        left = [jnp.where(live(s, j), panels[s][cols[0, s, j]], none) for j in range(slots)]
        left = jnp.concatenate(left, axis=1)
        right = jnp.concatenate([tiles[s][j] for j in range(slots)], axis=1)
        return lax.dot_general(
            left, right, (((1,), (1,)), ((), ())), preferred_element_type=jnp.float32
        )

    passed, handed = [], []
    for s in order:
        transposed(s)
        if s:
            c = remote(parts.at[s], landed.at[s - 1], p_send.at[s - 1], p_recv.at[s - 1], group(s))
            c.start()
            handed.append(c)

    for c in spread:
        c.wait_recv()
    for d in range(1, steps):
        c = remote(panels[0], panels[d], b_send.at[d - 1], b_recv.at[d - 1], group(-d))
        c.start()
        passed.append(c)

    summed = parts[0]
    for s in range(1, steps):
        handed[s - 1].wait_recv()
        summed += landed[s - 1]
    total[...] = summed
    returned = []
    for d in range(1, wide):
        to = owner(d)
        c = remote(total.at[to[1]], shares.at[d - 1], z_send.at[d - 1], z_recv.at[d - 1], to)
        c.start()
        returned.append(c)
    answer = direct(0) + total[w]
    for s in range(1, steps):
        passed[s - 1].wait_recv()
        answer += direct(s)
    for d in range(1, wide):
        returned[d - 1].wait_recv()
        answer += shares[d - 1]
    out[...] = answer
    for c in (*spread, *passed, *handed, *returned):
        c.wait_send()


def shards(mesh, vectors, blocks, columns, counts):
    groups, wide = mesh.shape["blk"], mesh.shape["wide"]
    vecs, size = vectors.shape
    _, steps, slots = blocks.shape[:3]
    sems = pltpu.SemaphoreType.DMA
    return pl.pallas_call(
        functools.partial(kernel, groups, wide, steps),
        out_shape=pltpu.VMEM((vecs, size), jnp.float32),
        in_specs=[pl.BlockSpec(memory_space=pltpu.HBM)] * 4,
        out_specs=pl.BlockSpec(memory_space=pltpu.VMEM),
        scratch_shapes=[
            *[pltpu.VMEM((wide, vecs, size), jnp.bfloat16)] * steps,
            *[pltpu.VMEM((slots, size, size), jnp.bfloat16)] * steps,
            pltpu.SMEM(columns.shape, jnp.int32),
            pltpu.SMEM(counts.shape, jnp.int32),
            pltpu.VMEM((vecs, size), jnp.bfloat16),
            pltpu.VMEM((steps, wide, vecs, size), jnp.float32),
            pltpu.VMEM((steps - 1, wide, vecs, size), jnp.float32),
            pltpu.VMEM((wide, vecs, size), jnp.float32),
            pltpu.VMEM((wide - 1, vecs, size), jnp.float32),
            sems((3,)),
            sems((steps,)),
            sems((wide - 1,)),
            sems((wide - 1,)),
            sems((steps - 1,)),
            sems((steps - 1,)),
            sems((steps - 1,)),
            sems((steps - 1,)),
            sems((wide - 1,)),
            sems((wide - 1,)),
        ],
        compiler_params=pltpu.CompilerParams(
            collective_id=0, has_side_effects=True, vmem_limit_bytes=60 << 20
        ),
    )(columns, counts, vectors, blocks)


def solution(mesh):
    return jax.shard_map(
        functools.partial(shards, mesh),
        mesh=mesh,
        in_specs=(
            P(None, ("blk", "wide")),
            P(("blk", "wide"), None, None, None, None),
            P(("blk", "wide"), None, None),
            P(("blk", "wide"), None),
        ),
        out_specs=P(None, ("blk", "wide")),
        check_vma=False,
    )
```
